32 devices in a mesh: groups: 2 (over y), seq: 8 (over z, x), ch: 2 (over core).
Axes of the slice: x: 2, y: 2, z: 4, core: 2. Of those that a mesh axis runs over, the one named last changes fastest.
Arguments:
- tokens: int32 [4096], P(('groups', 'seq')), parts along dimension 0, may hold values from 0 to 3
- nuc_table: bfloat16 [3, 4, 4096], P(None, None, 'ch'), may hold values from -6 to 6
- short_filter: float32 [3, 7, 4096], P(None, None, 'ch'), may hold values from -2 to 2
- mr_filter: float32 [256, 128], P('ch'), may hold values from -0.5 to 0.5
- head_weight: bfloat16 [5, 4096, 256], P(None, 'ch'), may hold values from -0.03125 to 0.03125
Outputs:
- annotation: bfloat16 [4096, 256], P(('groups', 'seq')), parts along dimension 0
The draws below stay inside these ranges and needn't reach their ends.
There are 2 independent parts, one for each index of `groups`. The reference program is written for one: setup_inputs(seed, part) draws one part's arguments, and reference() takes and returns one part's arrays. A program takes and returns all parts, laid end to end along the dimension named above; an argument that names none is the same for every part. Nothing has to cross between parts.
Inputs may be any that keep to these rules, and one draw needn't show every extreme that they name: `tokens`: each entry is a nucleotide letter: 0 A, 1 C, 2 G, 3 T; the complement of a is 3 - a. The letters are integers, so they may cross devices packed several to a 16-bit or wider word without losing anything.
All inputs are finite; a program needn't handle non-finite values.
Results may differ from the reference program's by a relative error of at most 0.0049.
Values may be sent and summed in bfloat16 or wider, within the bound.
A program may use at most 128 MiB of HBM per device.

```python
import jax
import jax.numpy as jnp
from jax import lax

D = 4096
GROUP = 16
TAPS_SHORT = 7
TAPS_MR = 128
TAPS_HEAD = 5
HEAD_OUT = 256
FILTERS = 256
LENGTH = 2048


def touch_ends(result, key, least, largest):
    shape = result.shape
    spot = [jax.random.randint(jax.random.fold_in(key, axis), (), 0, shape[axis]) for axis in range(len(shape))]
    result = result.at[tuple(spot)].set(least)
    longest = shape.index(max(shape))
    spot[longest] = (spot[longest] + 1) % shape[longest]
    return result.at[tuple(spot)].set(largest)


def shard_levels(key, dims, pieces, least, high):
    level, own = 1.0, jax.random.fold_in(key, 6)
    for position, parts in pieces:
        heights = jnp.exp(jax.random.uniform(jax.random.fold_in(own, position), (parts,), jnp.float32, least / len(pieces), high / len(pieces)))
        level = level * jnp.repeat(heights, dims[position] // parts).reshape([-1 if axis == position else 1 for axis in range(len(dims))])
    return level


def noise(rng, extent, width, bound, split=(), kind=jnp.bfloat16):
    gain = shard_levels(rng, extent, split, -0.22, 0.18) if split else 1.0
    entries = jax.random.normal(rng, extent, jnp.float32) * width * gain
    return jnp.minimum(jnp.maximum(entries, -bound), bound).astype(kind)


def setup_inputs(seed: int = 0, part: int = 0) -> dict:
    keys = jax.random.split(jax.random.key(seed), 6)
    part_keys = jax.random.split(jax.random.fold_in(keys[5], part), 6)
    tokens = touch_ends(jax.random.randint(part_keys[0], (LENGTH,), 0, 4), jax.random.fold_in(part_keys[0], 1), 0, 3).astype(jnp.int32)
    nuc_table = noise(keys[1], (3, 4, D), 1.0, 6.0, ((2, 2),))
    short_filter = noise(keys[2], (3, TAPS_SHORT, D), TAPS_SHORT ** -0.5, 2.0, ((2, 2),), jnp.float32)
    mr_filter = noise(keys[3], (FILTERS, TAPS_MR), TAPS_MR ** -0.5, 0.5, ((0, 2),), jnp.float32)
    head_weight = noise(keys[4], (TAPS_HEAD, D, HEAD_OUT), (2 * TAPS_HEAD * D) ** -0.5, 0.03125, ((1, 2),))
    return dict(tokens=tokens, nuc_table=nuc_table, short_filter=short_filter, mr_filter=mr_filter, head_weight=head_weight)


def causal_taps(stream, short_taps):
    short_len = short_taps.shape[0]
    out_count = stream.shape[1] - short_len + 1
    running = short_taps[0] * stream[:, short_len - 1: short_len - 1 + out_count]
    for lag_index in range(1, short_len):
        begin_row = short_len - 1 - lag_index
        running = running + short_taps[lag_index] * stream[:, begin_row: begin_row + out_count]
    return running


def toeplitz_rows(filters):
    group_count, filter_len = filters.shape
    padded = jnp.concatenate([jnp.zeros((group_count, 1), jnp.float32), filters[:, ::-1], jnp.zeros((group_count, filter_len), jnp.float32)], axis=1)
    tiled = jnp.tile(padded, (1, filter_len))[:, : 2 * filter_len * filter_len]
    return tiled.reshape(group_count, filter_len, 2 * filter_len)


def strand_block(onehot, nuc_block, short_taps, filters):
    filter_len = filters.shape[1]
    short_len = short_taps.shape[1]
    strands = onehot.shape[0]
    out_rows = onehot.shape[1] - (filter_len - 1) - (short_len - 1)
    channel_count = nuc_block.shape[2]
    group_count = filters.shape[0]
    lookup = jnp.einsum("sen,mnc->msec", onehot.astype(jnp.float32), nuc_block.astype(jnp.float32))
    query_rows = causal_taps(lookup[0, :, filter_len - 1:], short_taps[0])
    key_rows = causal_taps(lookup[1], short_taps[1])
    value_rows = causal_taps(lookup[2], short_taps[2])
    key_value = key_rows * value_rows
    padded = jnp.concatenate([jnp.zeros((strands, 1, channel_count), jnp.float32), key_value], axis=1)
    blocks = padded.reshape(strands, out_rows // filter_len + 1, filter_len, group_count, channel_count // group_count)
    paired = jnp.concatenate([blocks[:, :-1], blocks[:, 1:]], axis=2)
    matrix = toeplitz_rows(filters)
    mixed_rows = jnp.einsum("gij,snjgc->snigc", matrix, paired, precision=lax.Precision.HIGHEST)
    mixed_rows = mixed_rows.reshape(strands, out_rows, channel_count)
    return (query_rows * mixed_rows).astype(jnp.bfloat16)


def reference(tokens, nuc_table, short_filter, mr_filter, head_weight):
    filter_len = mr_filter.shape[1]
    short_len = short_filter.shape[1]
    rim_rows = filter_len - 1 + short_len - 1
    seq_length = tokens.shape[0]
    alphabet = jnp.arange(4, dtype=jnp.int32)
    strands = jnp.stack([tokens, 3 - tokens[::-1]])
    onehot = (strands[:, :, None] == alphabet).astype(jnp.float32)
    onehot = jnp.concatenate([jnp.zeros((2, rim_rows, 4), jnp.float32), onehot], axis=1)
    block_width = 256 if D % 256 == 0 else D
    block_count = D // block_width
    nuc_blocks = nuc_table.reshape(3, 4, block_count, block_width).transpose(2, 0, 1, 3)
    tap_blocks = short_filter.reshape(3, short_len, block_count, block_width).transpose(2, 0, 1, 3)
    mr_blocks = mr_filter.reshape(block_count, block_width // GROUP, filter_len)
    head_blocks = head_weight.reshape(TAPS_HEAD, block_count, block_width, HEAD_OUT).transpose(1, 0, 2, 3)
    head_rim = (TAPS_HEAD - 1) // 2

    def add_block(running, block_args):
        nuc_block, short_taps, filters, weight = block_args
        strand_track = strand_block(onehot, nuc_block, short_taps, filters)
        forward_pad = jnp.pad(strand_track[0], ((head_rim, head_rim), (0, 0)))
        reverse_pad = jnp.pad(strand_track[1][::-1], ((head_rim, head_rim), (0, 0)))
        for tap_index in range(TAPS_HEAD):
            mirror_row = TAPS_HEAD - 1 - tap_index
            running = running + jnp.dot(forward_pad[tap_index: tap_index + seq_length], weight[tap_index], preferred_element_type=jnp.float32)
            running = running + jnp.dot(reverse_pad[mirror_row: mirror_row + seq_length], weight[tap_index], preferred_element_type=jnp.float32)
        return running, None

    running, _ = lax.scan(add_block, jnp.zeros((seq_length, HEAD_OUT), jnp.float32), (nuc_blocks, tap_blocks, mr_blocks, head_blocks))
    return running.astype(jnp.bfloat16)
```

```python
import functools

import jax
import jax.numpy as jnp
from jax import lax
from jax.experimental import pallas as pl
from jax.experimental.pallas import tpu as pltpu
from jax.sharding import PartitionSpec as P

MESH = pl.DeviceIdType.MESH
CHUNK = 256


def dot(lhs, rhs, lhs_dim=1, rhs_dim=0):
    return lax.dot_general(
        lhs, rhs, (((lhs_dim,), (rhs_dim,)), ((), ())), preferred_element_type=jnp.float32
    )


def kernel(
    seq_count, tok_ref, nuc_ref, short_ref, mr_ref, head_hbm, out_ref,
    head, toeplitz, taps, short8, track, own, left_tok, right_tok, total, other, left_sum, right_sum,
    head_sem, tok_send, tok_recv, sum_send, sum_recv, rim_send, rim_recv,
):
    rows = tok_ref.shape[1]
    filters, span = mr_ref.shape
    channels = nuc_ref.shape[2]
    short_len = short_ref.shape[1]
    head_taps, _, outs = head.shape
    rim = (head_taps - 1) // 2
    width = channels // filters
    letters_count = nuc_ref.shape[1]
    pad = 8
    group = lax.axis_index("groups")
    place = lax.axis_index("seq")
    core = lax.axis_index("ch")
    has_left = place > 0
    has_right = place < seq_count - 1
    left = place - 1
    right = place + 1

    barrier = pltpu.get_barrier_semaphore()
    pl.semaphore_signal(barrier, inc=1, device_id=(group, place, 1 - core), device_id_type=MESH)

    @pl.when(has_left)
    def _():
        for c in range(2):
            pl.semaphore_signal(barrier, inc=1, device_id=(group, left, c), device_id_type=MESH)

    @pl.when(has_right)
    def _():
        for c in range(2):
            pl.semaphore_signal(barrier, inc=1, device_id=(group, right, c), device_id_type=MESH)

    head_copy = pltpu.make_async_copy(head_hbm, head, head_sem)
    head_copy.start()
    own[...] = jnp.broadcast_to(tok_ref[...], own.shape)
    count = 1 + 2 * has_left.astype(jnp.int32) + 2 * has_right.astype(jnp.int32)
    pl.semaphore_wait(barrier, count)

    def tok_copy(side):
        return pltpu.make_async_remote_copy(
            src_ref=own,
            dst_ref=right_tok if side == 0 else left_tok,
            send_sem=tok_send.at[side],
            recv_sem=tok_recv.at[side],
            device_id=(group, left if side == 0 else right, core),
            device_id_type=MESH,
        )

    @pl.when(has_left)
    def _():
        tok_copy(0).start()

    @pl.when(has_right)
    def _():
        tok_copy(1).start()

    for m in range(3):
        short8[0:short_len, :] = short_ref[m]
        short8[short_len:8, :] = jnp.zeros((8 - short_len, channels), jnp.float32)
        taps_f32 = short8[...]
        table = nuc_ref[m].astype(jnp.float32)
        full = jnp.concatenate([taps_f32 * table[n : n + 1] for n in range(letters_count)], axis=0)
        high = full.astype(jnp.bfloat16).astype(jnp.float32)
        both = jnp.concatenate([high, full - high], axis=0)
        taps[m] = both.T.astype(jnp.bfloat16)

    row_id = lax.broadcasted_iota(jnp.int32, (span, span), 0)
    lane_id = lax.broadcasted_iota(jnp.int32, (span, span), 1)

    def build(g, carry):
        wide = jnp.broadcast_to(mr_ref[pl.ds(g, 1), :], (span, span))
        circ = pltpu.roll(wide, 0, 1, stride=1, stride_axis=0)
        before = lane_id < row_id
        toeplitz[g, 0:span] = jnp.where(before, circ, 0.0).astype(jnp.bfloat16)
        toeplitz[g, span : 2 * span] = jnp.where(before, 0.0, circ).astype(jnp.bfloat16)
        return carry

    lax.fori_loop(0, filters, build, 0, unroll=4)

    @pl.when(has_left)
    def _():
        tok_copy(1).wait_recv()

    @pl.when(has_right)
    def _():
        tok_copy(0).wait_recv()

    @pl.when(jnp.logical_not(has_left))
    def _():
        left_tok[...] = jnp.full(left_tok.shape, -1, jnp.int32)

    @pl.when(jnp.logical_not(has_right))
    def _():
        right_tok[...] = jnp.full(right_tok.shape, -1, jnp.int32)

    mid = own[...].astype(jnp.float32)
    ahead = jnp.concatenate([left_tok[...].astype(jnp.float32), mid], axis=1)
    behind = jnp.concatenate([mid, right_tok[...].astype(jnp.float32)], axis=1)
    behind = (letters_count - 1) - behind
    flip = (row_id + lane_id == span - 1).astype(jnp.bfloat16)
    pieces = [
        dot(behind[:, p * span : (p + 1) * span].astype(jnp.bfloat16), flip)
        for p in reversed(range(2 * rows // span))
    ]
    behind = jnp.concatenate(pieces, axis=1)
    hots = []
    for line in (ahead, behind):
        lags = pltpu.roll(line, 0, 1, stride=1, stride_axis=0)[:, rows - span :]
        hot = jnp.concatenate([(lags == n).astype(jnp.float32) for n in range(letters_count)], axis=0)
        hots.append(jnp.concatenate([hot, hot], axis=0).astype(jnp.bfloat16))
    reach = rows + span
    hot_all = jnp.concatenate(hots, axis=1)
    hot_query = jnp.concatenate([h[:, span:] for h in hots], axis=1)
    blocks = rows // span
    perm_row = lax.broadcasted_iota(jnp.int32, (rows, rows), 0)
    perm_lane = lax.broadcasted_iota(jnp.int32, (rows, rows), 1)
    perms = [
        (perm_row == perm_lane).astype(jnp.bfloat16),
        (perm_row + perm_lane == rows - 1).astype(jnp.bfloat16),
    ]
    per_chunk = CHUNK // width

    def work(i, carry):
        at = pl.ds(pl.multiple_of(i * CHUNK, CHUNK), CHUNK)
        key = dot(taps[1, at, :], hot_all)
        value = dot(taps[2, at, :], hot_all)
        query = dot(taps[0, at, :], hot_query)
        gated = (key * value).astype(jnp.bfloat16)
        parts = []
        for g in range(per_chunk):
            lines = slice(g * width, (g + 1) * width)
            stack = jnp.concatenate(
                [
                    gated[lines, s * reach + b * span : s * reach + (b + 2) * span]
                    for s in range(2)
                    for b in range(blocks)
                ],
                axis=0,
            )
            mixed = dot(stack, toeplitz[i * per_chunk + g])
            mixed = jnp.concatenate(
                [mixed[n * width : (n + 1) * width] for n in range(2 * blocks)], axis=1
            )
            parts.append((query[lines] * mixed).astype(jnp.bfloat16))
        chunk_track = jnp.concatenate(parts, axis=0)
        for s in range(2):
            turned = dot(perms[s], chunk_track[:, s * rows : (s + 1) * rows], 1, 1)
            track[s, :, at] = turned.astype(jnp.bfloat16)
        return carry

    lax.fori_loop(0, channels // CHUNK, work, 0)

    head_copy.wait()
    total[...] = jnp.zeros_like(total)
    for d in range(head_taps):
        part = dot(track[0], head[d]) + dot(track[1], head[head_taps - 1 - d])
        begin = pad + rim - d
        total[begin : begin + rows, :] += part

    sum_copy = pltpu.make_async_remote_copy(
        src_ref=total.at[pl.ds(pad, rows)],
        dst_ref=other,
        send_sem=sum_send,
        recv_sem=sum_recv,
        device_id=(group, place, 1 - core),
        device_id_type=MESH,
    )
    sum_copy.start()

    def rim_copy(side, c, from_core):
        begin = 0 if side == 0 else pad + rows
        slots = right_sum if side == 0 else left_sum
        return pltpu.make_async_remote_copy(
            src_ref=total.at[pl.ds(begin, pad)],
            dst_ref=slots.at[from_core],
            send_sem=rim_send.at[side, c],
            recv_sem=rim_recv.at[side, from_core],
            device_id=(group, left if side == 0 else right, c),
            device_id_type=MESH,
        )

    @pl.when(has_left)
    def _():
        for c in range(2):
            rim_copy(0, c, core).start()

    @pl.when(has_right)
    def _():
        for c in range(2):
            rim_copy(1, c, core).start()

    @pl.when(jnp.logical_not(has_left))
    def _():
        left_sum[...] = jnp.zeros_like(left_sum)

    @pl.when(jnp.logical_not(has_right))
    def _():
        right_sum[...] = jnp.zeros_like(right_sum)

    @pl.when(has_left)
    def _():
        tok_copy(0).wait_send()
        for c in range(2):
            rim_copy(0, c, core).wait_send()
            rim_copy(1, 0, c).wait_recv()

    @pl.when(has_right)
    def _():
        tok_copy(1).wait_send()
        for c in range(2):
            rim_copy(1, c, core).wait_send()
            rim_copy(0, 0, c).wait_recv()

    sum_copy.wait()
    zero = jnp.zeros((pad - rim, outs), jnp.float32)
    lead = left_sum[0] + left_sum[1]
    trail = right_sum[0] + right_sum[1]
    line = lax.broadcasted_iota(jnp.int32, (pad, outs), 0)
    lead = jnp.where(line < rim, lead, 0.0)
    trail = jnp.where(line >= pad - rim, trail, 0.0)
    summed = total[pad : pad + rows, :] + other[...]
    del zero
    out_ref[0:16, :] = jnp.concatenate([summed[0:pad] + lead, summed[pad:16]], axis=0).astype(jnp.bfloat16)
    out_ref[16 : rows - 16, :] = summed[16 : rows - 16].astype(jnp.bfloat16)
    out_ref[rows - 16 : rows, :] = jnp.concatenate(
        [summed[rows - 16 : rows - pad], summed[rows - pad :] + trail], axis=0
    ).astype(jnp.bfloat16)


def shards(tokens, nuc_table, short_filter, mr_filter, head_weight):
    rows = tokens.shape[0]
    channels = nuc_table.shape[2]
    filters, span = mr_filter.shape
    outs = head_weight.shape[2]
    seq_count = lax.axis_size("seq")
    vmem = pl.BlockSpec(memory_space=pltpu.VMEM)
    pad = 8
    return pl.pallas_call(
        functools.partial(kernel, seq_count),
        out_shape=jax.ShapeDtypeStruct((rows, outs), jnp.bfloat16),
        in_specs=[vmem] * 4 + [pl.BlockSpec(memory_space=pl.ANY)],
        out_specs=vmem,
        scratch_shapes=[
            pltpu.VMEM(head_weight.shape, jnp.bfloat16),
            pltpu.VMEM((filters, 2 * span, span), jnp.bfloat16),
            pltpu.VMEM((3, channels, 64), jnp.bfloat16),
            pltpu.VMEM((8, channels), jnp.float32),
            pltpu.VMEM((2, rows, channels), jnp.bfloat16),
            pltpu.VMEM((8, rows), jnp.int32),
            pltpu.VMEM((8, rows), jnp.int32),
            pltpu.VMEM((8, rows), jnp.int32),
            pltpu.VMEM((rows + 2 * pad, outs), jnp.float32),
            pltpu.VMEM((rows, outs), jnp.float32),
            pltpu.VMEM((2, pad, outs), jnp.float32),
            pltpu.VMEM((2, pad, outs), jnp.float32),
            pltpu.SemaphoreType.DMA,
            pltpu.SemaphoreType.DMA((2,)),
            pltpu.SemaphoreType.DMA((2,)),
            pltpu.SemaphoreType.DMA,
            pltpu.SemaphoreType.DMA,
            pltpu.SemaphoreType.DMA((2, 2)),
            pltpu.SemaphoreType.DMA((2, 2)),
        ],
        compiler_params=pltpu.CompilerParams(
            collective_id=0, has_side_effects=True, vmem_limit_bytes=48 * 1024 * 1024
        ),
    )(tokens.reshape(1, rows), nuc_table, short_filter, mr_filter, head_weight)


def solution(mesh):
    in_specs = (
        P(("groups", "seq")),
        P(None, None, "ch"),
        P(None, None, "ch"),
        P("ch", None),
        P(None, "ch", None),
    )
    out_specs = P(("groups", "seq"), None)
    return jax.shard_map(shards, mesh=mesh, in_specs=in_specs, out_specs=out_specs, check_vma=False)
```

```python
import functools

import jax
import jax.numpy as jnp
from jax import lax
from jax.experimental import pallas as pl
from jax.experimental.pallas import tpu as pltpu
from jax.sharding import PartitionSpec as P

MESH = pl.DeviceIdType.MESH
CHUNK = 256


def dot(lhs, rhs, lhs_dim=1, rhs_dim=0):
    return lax.dot_general(
        lhs, rhs, (((lhs_dim,), (rhs_dim,)), ((), ())), preferred_element_type=jnp.float32
    )


def kernel(
    seq_count, tok_hbm, nuc_hbm, short_hbm, mr_hbm, head_hbm, out_ref,
    tok_ref, nuc_ref, short_ref, mr_ref, head, toeplitz, taps, short8, track, own, left_tok, right_tok, total, other, left_sum, right_sum,
    load_sem, tok_send, tok_recv, sum_send, sum_recv, rim_send, rim_recv,
):
    rows = tok_ref.shape[1]
    filters, span = mr_ref.shape
    channels = nuc_ref.shape[2]
    short_len = short_ref.shape[1]
    head_taps, _, outs = head.shape
    rim = (head_taps - 1) // 2
    width = channels // filters
    letters_count = nuc_ref.shape[1]
    pad = 8
    group = lax.axis_index("groups")
    place = lax.axis_index("seq")
    core = lax.axis_index("ch")
    has_left = place > 0
    has_right = place < seq_count - 1
    left = place - 1
    right = place + 1

    barrier = pltpu.get_barrier_semaphore()
    pl.semaphore_signal(barrier, inc=1, device_id=(group, place, 1 - core), device_id_type=MESH)

    @pl.when(has_left)
    def _():
        for c in range(2):
            pl.semaphore_signal(barrier, inc=1, device_id=(group, left, c), device_id_type=MESH)

    @pl.when(has_right)
    def _():
        for c in range(2):
            pl.semaphore_signal(barrier, inc=1, device_id=(group, right, c), device_id_type=MESH)

    loads = [
        pltpu.make_async_copy(source, target, load_sem.at[n])
        for n, (source, target) in enumerate(
            [(tok_hbm, tok_ref), (short_hbm, short_ref), (nuc_hbm, nuc_ref), (mr_hbm, mr_ref), (head_hbm, head)]
        )
    ]
    for load in loads:
        load.start()
    loads[0].wait()
    own[...] = jnp.broadcast_to(tok_ref[...], own.shape)
    loads[1].wait()
    loads[2].wait()
    for m in range(3):
        short8[0:short_len, :] = short_ref[m]
        short8[short_len:8, :] = jnp.zeros((8 - short_len, channels), jnp.float32)
        taps_f32 = short8[...]
        table = nuc_ref[m].astype(jnp.float32)
        full = jnp.concatenate([taps_f32 * table[n : n + 1] for n in range(letters_count)], axis=0)
        high = full.astype(jnp.bfloat16).astype(jnp.float32)
        both = jnp.concatenate([high, full - high], axis=0)
        taps[m] = both.T.astype(jnp.bfloat16)

    count = 1 + 2 * has_left.astype(jnp.int32) + 2 * has_right.astype(jnp.int32)
    pl.semaphore_wait(barrier, count)

    def tok_copy(side):
        return pltpu.make_async_remote_copy(
            src_ref=own,
            dst_ref=right_tok if side == 0 else left_tok,
            send_sem=tok_send.at[side],
            recv_sem=tok_recv.at[side],
            device_id=(group, left if side == 0 else right, core),
            device_id_type=MESH,
        )

    @pl.when(has_left)
    def _():
        tok_copy(0).start()

    @pl.when(has_right)
    def _():
        tok_copy(1).start()

    row_id = lax.broadcasted_iota(jnp.int32, (span, span), 0)
    lane_id = lax.broadcasted_iota(jnp.int32, (span, span), 1)

    loads[3].wait()
    before = (lane_id < row_id).astype(jnp.bfloat16)

    def build(g, carry):
        wide = jnp.broadcast_to(mr_ref[pl.ds(g, 1), :], (span, span))
        circ = pltpu.roll(wide, 0, 1, stride=1, stride_axis=0).astype(jnp.bfloat16)
        upper = circ * before
        toeplitz[g, 0:span] = upper
        toeplitz[g, span : 2 * span] = circ - upper
        return carry

    lax.fori_loop(0, filters, build, 0, unroll=4)

    @pl.when(has_left)
    def _():
        tok_copy(1).wait_recv()

    @pl.when(has_right)
    def _():
        tok_copy(0).wait_recv()

    @pl.when(jnp.logical_not(has_left))
    def _():
        left_tok[...] = jnp.full(left_tok.shape, -1, jnp.int32)

    @pl.when(jnp.logical_not(has_right))
    def _():
        right_tok[...] = jnp.full(right_tok.shape, -1, jnp.int32)

    mid = own[...].astype(jnp.float32)
    ahead = jnp.concatenate([left_tok[...].astype(jnp.float32), mid], axis=1)
    behind = jnp.concatenate([mid, right_tok[...].astype(jnp.float32)], axis=1)
    behind = (letters_count - 1) - behind
    flip = (row_id + lane_id == span - 1).astype(jnp.bfloat16)
    pieces = [
        dot(behind[:, p * span : (p + 1) * span].astype(jnp.bfloat16), flip)
        for p in reversed(range(2 * rows // span))
    ]
    behind = jnp.concatenate(pieces, axis=1)
    hots = []
    for line in (ahead, behind):
        lags = pltpu.roll(line, 0, 1, stride=1, stride_axis=0)[:, rows - span :]
        hot = jnp.concatenate([(lags == n).astype(jnp.float32) for n in range(letters_count)], axis=0)
        hots.append(jnp.concatenate([hot, hot], axis=0).astype(jnp.bfloat16))
    reach = rows + span
    hot_all = jnp.concatenate(hots, axis=1)
    hot_query = jnp.concatenate([h[:, span:] for h in hots], axis=1)
    blocks = rows // span
    perm_row = lax.broadcasted_iota(jnp.int32, (rows, rows), 0)
    perm_lane = lax.broadcasted_iota(jnp.int32, (rows, rows), 1)
    perms = [
        (perm_row == perm_lane).astype(jnp.bfloat16),
        (perm_row + perm_lane == rows - 1).astype(jnp.bfloat16),
    ]
    per_chunk = CHUNK // width

    def work(i, carry):
        at = pl.ds(pl.multiple_of(i * CHUNK, CHUNK), CHUNK)
        key = dot(taps[1, at, :], hot_all)
        value = dot(taps[2, at, :], hot_all)
        query = dot(taps[0, at, :], hot_query)
        gated = (key * value).astype(jnp.bfloat16)
        parts = []
        for g in range(per_chunk):
            lines = slice(g * width, (g + 1) * width)
            stack = jnp.concatenate(
                [
                    gated[lines, s * reach + b * span : s * reach + (b + 2) * span]
                    for s in range(2)
                    for b in range(blocks)
                ],
                axis=0,
            )
            mixed = dot(stack, toeplitz[i * per_chunk + g])
            mixed = jnp.concatenate(
                [mixed[n * width : (n + 1) * width] for n in range(2 * blocks)], axis=1
            )
            parts.append((query[lines] * mixed).astype(jnp.bfloat16))
        chunk_track = jnp.concatenate(parts, axis=0)
        for s in range(2):
            turned = dot(perms[s], chunk_track[:, s * rows : (s + 1) * rows], 1, 1)
            track[s, :, at] = turned.astype(jnp.bfloat16)
        return carry

    lax.fori_loop(0, channels // CHUNK, work, 0, unroll=True)

    loads[4].wait()
    total[...] = jnp.zeros_like(total)
    half = rows // 2
    cut = pad + half - 8

    def sum_copy(part):
        lines = pl.ds(pad, cut - pad) if part == 0 else pl.ds(cut, rows + pad - cut)
        return pltpu.make_async_remote_copy(
            src_ref=total.at[lines],
            dst_ref=other.at[lines],
            send_sem=sum_send.at[part],
            recv_sem=sum_recv.at[part],
            device_id=(group, place, 1 - core),
            device_id_type=MESH,
        )

    def rim_copy(side, c, from_core):
        begin = 0 if side == 0 else pad + rows
        slots = right_sum if side == 0 else left_sum
        return pltpu.make_async_remote_copy(
            src_ref=total.at[pl.ds(begin, pad)],
            dst_ref=slots.at[from_core],
            send_sem=rim_send.at[side, c],
            recv_sem=rim_recv.at[side, from_core],
            device_id=(group, left if side == 0 else right, c),
            device_id_type=MESH,
        )

    for part in range(2):
        for d in range(head_taps):
            lines = slice(part * half, (part + 1) * half)
            term = dot(track[0, lines], head[d]) + dot(track[1, lines], head[head_taps - 1 - d])
            begin = pad + rim - d + part * half
            total[begin : begin + half, :] += term
        sum_copy(part).start()

        @pl.when(has_left if part == 0 else has_right)
        def _():
            for c in range(2):
                rim_copy(part, c, core).start()

    @pl.when(jnp.logical_not(has_left))
    def _():
        left_sum[...] = jnp.zeros_like(left_sum)

    @pl.when(jnp.logical_not(has_right))
    def _():
        right_sum[...] = jnp.zeros_like(right_sum)

    @pl.when(has_left)
    def _():
        tok_copy(0).wait_send()
        for c in range(2):
            rim_copy(0, c, core).wait_send()
            rim_copy(1, 0, c).wait_recv()

    @pl.when(has_right)
    def _():
        tok_copy(1).wait_send()
        for c in range(2):
            rim_copy(1, c, core).wait_send()
            rim_copy(0, 0, c).wait_recv()

    sum_copy(0).wait()
    sum_copy(1).wait()
    lead = left_sum[0] + left_sum[1]
    trail = right_sum[0] + right_sum[1]
    summed = total[pad : pad + rows, :] + other[pad : pad + rows, :]
    out_ref[0:16, :] = jnp.concatenate([summed[0:pad] + lead, summed[pad:16]], axis=0).astype(jnp.bfloat16)
    out_ref[16 : rows - 16, :] = summed[16 : rows - 16].astype(jnp.bfloat16)
    out_ref[rows - 16 : rows, :] = jnp.concatenate(
        [summed[rows - 16 : rows - pad], summed[rows - pad :] + trail], axis=0
    ).astype(jnp.bfloat16)


def shards(tokens, nuc_table, short_filter, mr_filter, head_weight):
    rows = tokens.shape[0]
    channels = nuc_table.shape[2]
    filters, span = mr_filter.shape
    outs = head_weight.shape[2]
    seq_count = lax.axis_size("seq")
    vmem = pl.BlockSpec(memory_space=pltpu.VMEM)
    pad = 8
    return pl.pallas_call(
        functools.partial(kernel, seq_count),
        out_shape=jax.ShapeDtypeStruct((rows, outs), jnp.bfloat16),
        in_specs=[pl.BlockSpec(memory_space=pltpu.HBM)] * 5,
        out_specs=vmem,
        scratch_shapes=[
            pltpu.VMEM((1, rows), jnp.int32),
            pltpu.VMEM(nuc_table.shape, jnp.bfloat16),
            pltpu.VMEM(short_filter.shape, jnp.float32),
            pltpu.VMEM(mr_filter.shape, jnp.float32),
            pltpu.VMEM(head_weight.shape, jnp.bfloat16),
            pltpu.VMEM((filters, 2 * span, span), jnp.bfloat16),
            pltpu.VMEM((3, channels, 64), jnp.bfloat16),
            pltpu.VMEM((8, channels), jnp.float32),
            pltpu.VMEM((2, rows, channels), jnp.bfloat16),
            pltpu.VMEM((8, rows), jnp.int32),
            pltpu.VMEM((8, rows), jnp.int32),
            pltpu.VMEM((8, rows), jnp.int32),
            pltpu.VMEM((rows + 2 * pad, outs), jnp.float32),
            pltpu.VMEM((rows + 2 * pad, outs), jnp.float32),
            pltpu.VMEM((2, pad, outs), jnp.float32),
            pltpu.VMEM((2, pad, outs), jnp.float32),
            pltpu.SemaphoreType.DMA((5,)),
            pltpu.SemaphoreType.DMA((2,)),
            pltpu.SemaphoreType.DMA((2,)),
            pltpu.SemaphoreType.DMA((2,)),
            pltpu.SemaphoreType.DMA((2,)),
            pltpu.SemaphoreType.DMA((2, 2)),
            pltpu.SemaphoreType.DMA((2, 2)),
        ],
        compiler_params=pltpu.CompilerParams(
            collective_id=0, has_side_effects=True, vmem_limit_bytes=63 * 1024 * 1024
        ),
    )(tokens.reshape(1, rows), nuc_table, short_filter, mr_filter, head_weight)


def solution(mesh):
    in_specs = (
        P(("groups", "seq")),
        P(None, None, "ch"),
        P(None, None, "ch"),
        P("ch", None),
        P(None, "ch", None),
    )
    out_specs = P(("groups", "seq"), None)
    return jax.shard_map(shards, mesh=mesh, in_specs=in_specs, out_specs=out_specs, check_vma=False)
```

```python
import functools

import jax
import jax.numpy as jnp
from jax import lax
from jax.experimental import pallas as pl
from jax.experimental.pallas import tpu as pltpu
from jax.sharding import PartitionSpec as P

MESH = pl.DeviceIdType.MESH


def dot(lhs, rhs, lhs_dim=1, rhs_dim=0):
    return lax.dot_general(
        lhs, rhs, (((lhs_dim,), (rhs_dim,)), ((), ())), preferred_element_type=jnp.float32
    )


def kernel(
    seq_count, tok_hbm, nuc_hbm, short_hbm, mr_hbm, head_hbm, out_ref,
    tok_ref, nuc_ref, short_ref, mr_ref, head, toeplitz, taps, short8, track, own, left_tok, right_tok, total, other, left_sum, right_sum,
    load_sem, tok_send, tok_recv, sum_send, sum_recv, rim_send, rim_recv,
):
    rows = tok_ref.shape[1]
    filters, span = mr_ref.shape
    channels = nuc_ref.shape[2]
    short_len = short_ref.shape[1]
    head_taps, _, outs = head.shape
    rim = (head_taps - 1) // 2
    width = channels // filters
    letters_count = nuc_ref.shape[1]
    pad = 8
    group = lax.axis_index("groups")
    place = lax.axis_index("seq")
    core = lax.axis_index("ch")
    has_left = place > 0
    has_right = place < seq_count - 1
    left = place - 1
    right = place + 1

    barrier = pltpu.get_barrier_semaphore()
    pl.semaphore_signal(barrier, inc=1, device_id=(group, place, 1 - core), device_id_type=MESH)

    @pl.when(has_left)
    def _():
        for c in range(2):
            pl.semaphore_signal(barrier, inc=1, device_id=(group, left, c), device_id_type=MESH)

    @pl.when(has_right)
    def _():
        for c in range(2):
            pl.semaphore_signal(barrier, inc=1, device_id=(group, right, c), device_id_type=MESH)

    loads = [
        pltpu.make_async_copy(source, target, load_sem.at[n])
        for n, (source, target) in enumerate(
            [(tok_hbm, tok_ref), (short_hbm, short_ref), (nuc_hbm, nuc_ref), (mr_hbm, mr_ref), (head_hbm, head)]
        )
    ]
    for load in loads:
        load.start()
    loads[0].wait()
    own[...] = jnp.broadcast_to(tok_ref[...], own.shape)
    loads[1].wait()
    loads[2].wait()
    for m in range(3):
        short8[0:short_len, :] = short_ref[m]
        short8[short_len:8, :] = jnp.zeros((8 - short_len, channels), jnp.float32)
        taps_f32 = short8[...]
        table = nuc_ref[m].astype(jnp.float32)
        full = jnp.concatenate([taps_f32 * table[n : n + 1] for n in range(letters_count)], axis=0)
        high = full.astype(jnp.bfloat16).astype(jnp.float32)
        both = jnp.concatenate([high, full - high], axis=0)
        taps[m] = both.T.astype(jnp.bfloat16)

    count = 1 + 2 * has_left.astype(jnp.int32) + 2 * has_right.astype(jnp.int32)
    pl.semaphore_wait(barrier, count)

    def tok_copy(side):
        return pltpu.make_async_remote_copy(
            src_ref=own,
            dst_ref=right_tok if side == 0 else left_tok,
            send_sem=tok_send.at[side],
            recv_sem=tok_recv.at[side],
            device_id=(group, left if side == 0 else right, core),
            device_id_type=MESH,
        )

    @pl.when(has_left)
    def _():
        tok_copy(0).start()

    @pl.when(has_right)
    def _():
        tok_copy(1).start()

    row_id = lax.broadcasted_iota(jnp.int32, (span, span), 0)
    lane_id = lax.broadcasted_iota(jnp.int32, (span, span), 1)

    loads[3].wait()
    before = (lane_id < row_id).astype(jnp.bfloat16)

    def build(g, carry):
        wide = jnp.broadcast_to(mr_ref[pl.ds(g, 1), :], (span, span))
        circ = pltpu.roll(wide, 0, 1, stride=1, stride_axis=0).astype(jnp.bfloat16)
        upper = circ * before
        toeplitz[g, 0:span] = upper
        toeplitz[g, span : 2 * span] = circ - upper
        return carry

    lax.fori_loop(0, filters, build, 0, unroll=16)

    @pl.when(has_left)
    def _():
        tok_copy(1).wait_recv()

    @pl.when(has_right)
    def _():
        tok_copy(0).wait_recv()

    @pl.when(jnp.logical_not(has_left))
    def _():
        left_tok[...] = jnp.full(left_tok.shape, -1, jnp.int32)

    @pl.when(jnp.logical_not(has_right))
    def _():
        right_tok[...] = jnp.full(right_tok.shape, -1, jnp.int32)

    mid = own[...].astype(jnp.float32)
    ahead = jnp.concatenate([left_tok[...].astype(jnp.float32), mid], axis=1)
    behind = jnp.concatenate([mid, right_tok[...].astype(jnp.float32)], axis=1)
    behind = (letters_count - 1) - behind
    flip = (row_id + lane_id == span - 1).astype(jnp.bfloat16)
    pieces = [
        dot(behind[:, p * span : (p + 1) * span].astype(jnp.bfloat16), flip)
        for p in reversed(range(2 * rows // span))
    ]
    behind = jnp.concatenate(pieces, axis=1)
    hots = []
    for line in (ahead, behind):
        lags = pltpu.roll(line, 0, 1, stride=1, stride_axis=0)[:, rows - span :]
        hot = jnp.concatenate([(lags == n).astype(jnp.float32) for n in range(letters_count)], axis=0)
        hots.append(jnp.concatenate([hot, hot], axis=0).astype(jnp.bfloat16))
    reach = rows + span
    hot_all = jnp.concatenate(hots, axis=1)
    hot_query = jnp.concatenate([h[:, span:] for h in hots], axis=1)
    wide = 2 * span
    hot_tiles = [hot_all[:, t : t + wide] for t in range(0, 2 * reach, wide)]
    query_tiles = [hot_query[:, t : t + wide] for t in range(0, 2 * rows, wide)]
    blocks = rows // span
    perm_row = lax.broadcasted_iota(jnp.int32, (rows, rows), 0)
    perm_lane = lax.broadcasted_iota(jnp.int32, (rows, rows), 1)
    perms = [
        (perm_row == perm_lane).astype(jnp.bfloat16),
        (perm_row + perm_lane == rows - 1).astype(jnp.bfloat16),
    ]
    part_channels = span
    per_part = part_channels // width
    half = rows // 2

    def gate(p):
        at = slice(p * part_channels, (p + 1) * part_channels)
        cells = []
        for hot in hot_tiles:
            gated = (dot(taps[1, at, :], hot) * dot(taps[2, at, :], hot)).astype(jnp.bfloat16)
            cells += [gated[:, t : t + span] for t in range(0, hot.shape[1], span)]
        return cells

    def mix(p, cells):
        at = slice(p * part_channels, (p + 1) * part_channels)
        query = jnp.concatenate([dot(taps[0, at, :], hot) for hot in query_tiles], axis=1)
        parts = []
        for g in range(per_part):
            lines = slice(g * width, (g + 1) * width)
            stack = jnp.concatenate(
                [
                    jnp.concatenate(
                        [cells[s * (blocks + 1) + b][lines], cells[s * (blocks + 1) + b + 1][lines]], axis=1
                    )
                    for s in range(2)
                    for b in range(blocks)
                ],
                axis=0,
            )
            mixed = dot(stack, toeplitz[p * per_part + g])
            mixed = jnp.concatenate(
                [mixed[n * width : (n + 1) * width] for n in range(2 * blocks)], axis=1
            )
            parts.append((query[lines] * mixed).astype(jnp.bfloat16))
        return jnp.concatenate(parts, axis=0)

    def turn(begin, tracks):
        chunk_track = jnp.concatenate(tracks, axis=0)
        at = slice(begin * part_channels, (begin + len(tracks)) * part_channels)
        for s in range(2):
            turned = dot(perms[s], chunk_track[:, s * rows : (s + 1) * rows], 1, 1).astype(jnp.bfloat16)
            for h in range(2):
                track[h, s * half : (s + 1) * half, at] = turned[h * half : (h + 1) * half]

    part_count = channels // part_channels
    pending = []
    cells = gate(0)
    for p in range(part_count):
        ahead_cells = gate(p + 1) if p + 1 < part_count else None
        done = mix(p, cells)
        cells = ahead_cells
        pending.append(done)
        if len(pending) == 3:
            turn(p - 2, pending[:2])
            pending = pending[2:]
    turn(part_count - len(pending), pending)

    loads[4].wait()
    total[...] = jnp.zeros_like(total)
    cut = pad + half - 8

    def sum_copy(part):
        lines = pl.ds(pad, cut - pad) if part == 0 else pl.ds(cut, rows + pad - cut)
        return pltpu.make_async_remote_copy(
            src_ref=total.at[lines],
            dst_ref=other.at[lines],
            send_sem=sum_send.at[part],
            recv_sem=sum_recv.at[part],
            device_id=(group, place, 1 - core),
            device_id_type=MESH,
        )

    def rim_copy(side, c, from_core):
        begin = 0 if side == 0 else pad + rows
        slots = right_sum if side == 0 else left_sum
        return pltpu.make_async_remote_copy(
            src_ref=total.at[pl.ds(begin, pad)],
            dst_ref=slots.at[from_core],
            send_sem=rim_send.at[side, c],
            recv_sem=rim_recv.at[side, from_core],
            device_id=(group, left if side == 0 else right, c),
            device_id_type=MESH,
        )

    for part in range(2):
        for d in range(head_taps):
            term = dot(track[part], head[d])
            begin = pad + rim - d + part * half
            total[begin : begin + half, :] += term[:half]
            begin = pad + d - rim + part * half
            total[begin : begin + half, :] += term[half:]
        sum_copy(part).start()

        @pl.when(has_left if part == 0 else has_right)
        def _():
            for c in range(2):
                rim_copy(part, c, core).start()

    @pl.when(jnp.logical_not(has_left))
    def _():
        left_sum[...] = jnp.zeros_like(left_sum)

    @pl.when(jnp.logical_not(has_right))
    def _():
        right_sum[...] = jnp.zeros_like(right_sum)

    @pl.when(has_left)
    def _():
        tok_copy(0).wait_send()
        for c in range(2):
            rim_copy(0, c, core).wait_send()
            rim_copy(1, 0, c).wait_recv()

    @pl.when(has_right)
    def _():
        tok_copy(1).wait_send()
        for c in range(2):
            rim_copy(1, c, core).wait_send()
            rim_copy(0, 0, c).wait_recv()

    sum_copy(0).wait()
    sum_copy(1).wait()
    lead = left_sum[0] + left_sum[1]
    trail = right_sum[0] + right_sum[1]
    summed = total[pad : pad + rows, :] + other[pad : pad + rows, :]
    out_ref[0:pad, :] = summed[0:pad] + lead
    out_ref[pad : rows - pad, :] = summed[pad : rows - pad]
    out_ref[rows - pad : rows, :] = summed[rows - pad : rows] + trail


def shards(tokens, nuc_table, short_filter, mr_filter, head_weight):
    rows = tokens.shape[0]
    channels = nuc_table.shape[2]
    filters, span = mr_filter.shape
    outs = head_weight.shape[2]
    seq_count = lax.axis_size("seq")
    vmem = pl.BlockSpec(memory_space=pltpu.VMEM)
    pad = 8
    return pl.pallas_call(
        functools.partial(kernel, seq_count),
        out_shape=jax.ShapeDtypeStruct((rows, outs), jnp.float32),
        in_specs=[pl.BlockSpec(memory_space=pltpu.HBM)] * 5,
        out_specs=vmem,
        scratch_shapes=[
            pltpu.VMEM((1, rows), jnp.int32),
            pltpu.VMEM(nuc_table.shape, jnp.bfloat16),
            pltpu.VMEM(short_filter.shape, jnp.float32),
            pltpu.VMEM(mr_filter.shape, jnp.float32),
            pltpu.VMEM(head_weight.shape, jnp.bfloat16),
            pltpu.VMEM((filters, 2 * span, span), jnp.bfloat16),
            pltpu.VMEM((3, channels, 64), jnp.bfloat16),
            pltpu.VMEM((8, channels), jnp.float32),
            pltpu.VMEM((2, rows, channels), jnp.bfloat16),
            pltpu.VMEM((8, rows), jnp.int32),
            pltpu.VMEM((8, rows), jnp.int32),
            pltpu.VMEM((8, rows), jnp.int32),
            pltpu.VMEM((rows + 2 * pad, outs), jnp.float32),
            pltpu.VMEM((rows + 2 * pad, outs), jnp.float32),
            pltpu.VMEM((2, pad, outs), jnp.float32),
            pltpu.VMEM((2, pad, outs), jnp.float32),
            pltpu.SemaphoreType.DMA((5,)),
            pltpu.SemaphoreType.DMA((2,)),
            pltpu.SemaphoreType.DMA((2,)),
            pltpu.SemaphoreType.DMA((2,)),
            pltpu.SemaphoreType.DMA((2,)),
            pltpu.SemaphoreType.DMA((2, 2)),
            pltpu.SemaphoreType.DMA((2, 2)),
        ],
        compiler_params=pltpu.CompilerParams(
            collective_id=0, has_side_effects=True, vmem_limit_bytes=63 * 1024 * 1024
        ),
    )(tokens.reshape(1, rows), nuc_table, short_filter, mr_filter, head_weight).astype(jnp.bfloat16)


def solution(mesh):
    in_specs = (
        P(("groups", "seq")),
        P(None, None, "ch"),
        P(None, None, "ch"),
        P("ch", None),
        P(None, "ch", None),
    )
    out_specs = P(("groups", "seq"), None)
    return jax.shard_map(shards, mesh=mesh, in_specs=in_specs, out_specs=out_specs, check_vma=False)
```

```python
import functools

import jax
import jax.numpy as jnp
from jax import lax
from jax.experimental import pallas as pl
from jax.experimental.pallas import tpu as pltpu
from jax.sharding import PartitionSpec as P

MESH = pl.DeviceIdType.MESH


def dot(lhs, rhs, lhs_dim=1, rhs_dim=0):
    return lax.dot_general(
        lhs, rhs, (((lhs_dim,), (rhs_dim,)), ((), ())), preferred_element_type=jnp.float32
    )


def kernel(
    seq_count, tok_hbm, nuc_hbm, short_hbm, mr_hbm, head_hbm, out_ref,
    tok_ref, nuc_ref, short_ref, mr_ref, head, toeplitz, taps, short8, track, own, left_tok, right_tok, total, other, left_sum, right_sum,
    load_sem, tok_send, tok_recv, sum_send, sum_recv, rim_send, rim_recv,
):
    rows = tok_ref.shape[1]
    filters, span = mr_ref.shape
    channels = nuc_ref.shape[2]
    short_len = short_ref.shape[1]
    head_taps, _, outs = head.shape
    rim = (head_taps - 1) // 2
    width = channels // filters
    letters_count = nuc_ref.shape[1]
    pad = 8
    group = lax.axis_index("groups")
    place = lax.axis_index("seq")
    core = lax.axis_index("ch")
    has_left = place > 0
    has_right = place < seq_count - 1
    left = place - 1
    right = place + 1

    barrier = pltpu.get_barrier_semaphore()
    pl.semaphore_signal(barrier, inc=1, device_id=(group, place, 1 - core), device_id_type=MESH)

    @pl.when(has_left)
    def _():
        for c in range(2):
            pl.semaphore_signal(barrier, inc=1, device_id=(group, left, c), device_id_type=MESH)

    @pl.when(has_right)
    def _():
        for c in range(2):
            pl.semaphore_signal(barrier, inc=1, device_id=(group, right, c), device_id_type=MESH)

    loads = [
        pltpu.make_async_copy(source, target, load_sem.at[n])
        for n, (source, target) in enumerate(
            [(tok_hbm, tok_ref), (short_hbm, short_ref), (nuc_hbm, nuc_ref), (mr_hbm, mr_ref), (head_hbm, head)]
        )
    ]
    for load in loads:
        load.start()
    loads[0].wait()
    own[...] = jnp.broadcast_to(tok_ref[...], own.shape)
    loads[1].wait()
    loads[2].wait()
    for m in range(3):
        short8[0:short_len, :] = short_ref[m]
        short8[short_len:8, :] = jnp.zeros((8 - short_len, channels), jnp.float32)
        taps_f32 = short8[...]
        table = nuc_ref[m].astype(jnp.float32)
        full = jnp.concatenate([taps_f32 * table[n : n + 1] for n in range(letters_count)], axis=0)
        high = full.astype(jnp.bfloat16).astype(jnp.float32)
        both = jnp.concatenate([high, full - high], axis=0)
        taps[m] = both.T.astype(jnp.bfloat16)

    count = 1 + 2 * has_left.astype(jnp.int32) + 2 * has_right.astype(jnp.int32)
    pl.semaphore_wait(barrier, count)

    def tok_copy(side):
        return pltpu.make_async_remote_copy(
            src_ref=own,
            dst_ref=right_tok if side == 0 else left_tok,
            send_sem=tok_send.at[side],
            recv_sem=tok_recv.at[side],
            device_id=(group, left if side == 0 else right, core),
            device_id_type=MESH,
        )

    @pl.when(has_left)
    def _():
        tok_copy(0).start()

    @pl.when(has_right)
    def _():
        tok_copy(1).start()

    row_id = lax.broadcasted_iota(jnp.int32, (span, span), 0)
    lane_id = lax.broadcasted_iota(jnp.int32, (span, span), 1)

    loads[3].wait()
    before = (lane_id < row_id).astype(jnp.bfloat16)

    part_channels = span
    part_count = channels // part_channels
    per_part = part_channels // width
    early_parts = part_count // 2

    def build(g):
        base = pltpu.roll(jnp.broadcast_to(mr_ref[pl.ds(g, 1), :], (8, span)), 0, 1, stride=1, stride_axis=0)
        turns = [base] + [pltpu.roll(base, n, 1) for n in range(8, span, 8)]
        circ = jnp.concatenate(turns, axis=0).astype(jnp.bfloat16)
        upper = circ * before
        toeplitz[g, 0:span] = upper
        toeplitz[g, span : 2 * span] = circ - upper

    def build_step(p, carry):
        for g in range(per_part):
            build(p * per_part + g)
        return carry

    lax.fori_loop(0, early_parts, build_step, 0)

    @pl.when(has_left)
    def _():
        tok_copy(1).wait_recv()

    @pl.when(has_right)
    def _():
        tok_copy(0).wait_recv()

    @pl.when(jnp.logical_not(has_left))
    def _():
        left_tok[...] = jnp.full(left_tok.shape, -1, jnp.int32)

    @pl.when(jnp.logical_not(has_right))
    def _():
        right_tok[...] = jnp.full(right_tok.shape, -1, jnp.int32)

    mid = own[...].astype(jnp.float32)
    ahead = jnp.concatenate([left_tok[...].astype(jnp.float32), mid], axis=1)
    behind = jnp.concatenate([mid, right_tok[...].astype(jnp.float32)], axis=1)
    behind = (letters_count - 1) - behind
    flip = (row_id + lane_id == span - 1).astype(jnp.bfloat16)
    pieces = [
        dot(behind[:, p * span : (p + 1) * span].astype(jnp.bfloat16), flip)
        for p in reversed(range(2 * rows // span))
    ]
    behind = jnp.concatenate(pieces, axis=1)
    hots = []
    for line in (ahead, behind):
        lags = pltpu.roll(line, 0, 1, stride=1, stride_axis=0)[:, rows - span :]
        hot = jnp.concatenate([(lags == n).astype(jnp.float32) for n in range(letters_count)], axis=0)
        hots.append(jnp.concatenate([hot, hot], axis=0).astype(jnp.bfloat16))
    reach = rows + span
    hot_all = jnp.concatenate(hots, axis=1)
    hot_query = jnp.concatenate([h[:, span:] for h in hots], axis=1)
    wide = 2 * span
    hot_tiles = [hot_all[:, t : t + wide] for t in range(0, 2 * reach, wide)]
    query_tiles = [hot_query[:, t : t + wide] for t in range(0, 2 * rows, wide)]
    blocks = rows // span
    perm_row = lax.broadcasted_iota(jnp.int32, (rows, rows), 0)
    perm_lane = lax.broadcasted_iota(jnp.int32, (rows, rows), 1)
    perms = [
        (perm_row == perm_lane).astype(jnp.bfloat16),
        (perm_row + perm_lane == rows - 1).astype(jnp.bfloat16),
    ]
    half = rows // 2

    def gate(p):
        at = slice(p * part_channels, (p + 1) * part_channels)
        cells = []
        for hot in hot_tiles:
            gated = (dot(taps[1, at, :], hot) * dot(taps[2, at, :], hot)).astype(jnp.bfloat16)
            cells += [gated[:, t : t + span] for t in range(0, hot.shape[1], span)]
        return cells

    def mix(p, cells):
        at = slice(p * part_channels, (p + 1) * part_channels)
        query = jnp.concatenate([dot(taps[0, at, :], hot) for hot in query_tiles], axis=1)
        parts = []
        for g in range(per_part):
            lines = slice(g * width, (g + 1) * width)
            stack = jnp.concatenate(
                [
                    jnp.concatenate(
                        [cells[s * (blocks + 1) + b][lines], cells[s * (blocks + 1) + b + 1][lines]], axis=1
                    )
                    for s in range(2)
                    for b in range(blocks)
                ],
                axis=0,
            )
            mixed = dot(stack, toeplitz[p * per_part + g])
            mixed = jnp.concatenate(
                [mixed[n * width : (n + 1) * width] for n in range(2 * blocks)], axis=1
            )
            parts.append((query[lines] * mixed).astype(jnp.bfloat16))
        return jnp.concatenate(parts, axis=0)

    def turn(begin, tracks):
        chunk_track = jnp.concatenate(tracks, axis=0)
        at = slice(begin * part_channels, (begin + len(tracks)) * part_channels)
        for s in range(2):
            turned = dot(perms[s], chunk_track[:, s * rows : (s + 1) * rows], 1, 1).astype(jnp.bfloat16)
            for h in range(2):
                track[h, s * half : (s + 1) * half, at] = turned[h * half : (h + 1) * half]

    pending = []
    cells = gate(0)
    for p in range(part_count):
        ahead_cells = gate(p + 1) if p + 1 < part_count else None
        if p + early_parts < part_count:
            for g in range(per_part):
                build((p + early_parts) * per_part + g)
        done = mix(p, cells)
        cells = ahead_cells
        pending.append(done)
        if len(pending) == 3:
            turn(p - 2, pending[:2])
            pending = pending[2:]
    turn(part_count - len(pending), pending)

    loads[4].wait()
    total[...] = jnp.zeros_like(total)
    cut = pad + half - 8

    def sum_copy(part):
        lines = pl.ds(pad, cut - pad) if part == 0 else pl.ds(cut, rows + pad - cut)
        return pltpu.make_async_remote_copy(
            src_ref=total.at[lines],
            dst_ref=other.at[lines],
            send_sem=sum_send.at[part],
            recv_sem=sum_recv.at[part],
            device_id=(group, place, 1 - core),
            device_id_type=MESH,
        )

    def rim_copy(side, c, from_core):
        begin = 0 if side == 0 else pad + rows
        slots = right_sum if side == 0 else left_sum
        return pltpu.make_async_remote_copy(
            src_ref=total.at[pl.ds(begin, pad)],
            dst_ref=slots.at[from_core],
            send_sem=rim_send.at[side, c],
            recv_sem=rim_recv.at[side, from_core],
            device_id=(group, left if side == 0 else right, c),
            device_id_type=MESH,
        )

    for part in range(2):
        for d in range(head_taps):
            term = dot(track[part], head[d])
            begin = pad + rim - d + part * half
            total[begin : begin + half, :] += term[:half]
            begin = pad + d - rim + part * half
            total[begin : begin + half, :] += term[half:]
        sum_copy(part).start()

        @pl.when(has_left if part == 0 else has_right)
        def _():
            for c in range(2):
                rim_copy(part, c, core).start()

    @pl.when(jnp.logical_not(has_left))
    def _():
        left_sum[...] = jnp.zeros_like(left_sum)

    @pl.when(jnp.logical_not(has_right))
    def _():
        right_sum[...] = jnp.zeros_like(right_sum)

    @pl.when(has_left)
    def _():
        tok_copy(0).wait_send()
        for c in range(2):
            rim_copy(0, c, core).wait_send()
            rim_copy(1, 0, c).wait_recv()

    @pl.when(has_right)
    def _():
        tok_copy(1).wait_send()
        for c in range(2):
            rim_copy(1, c, core).wait_send()
            rim_copy(0, 0, c).wait_recv()

    sum_copy(0).wait()
    sum_copy(1).wait()
    lead = left_sum[0] + left_sum[1]
    trail = right_sum[0] + right_sum[1]
    summed = total[pad : pad + rows, :] + other[pad : pad + rows, :]
    out_ref[0:16, :] = jnp.concatenate([summed[0:pad] + lead, summed[pad:16]], axis=0).astype(jnp.bfloat16)
    out_ref[16 : rows - 16, :] = summed[16 : rows - 16].astype(jnp.bfloat16)
    out_ref[rows - 16 : rows, :] = jnp.concatenate(
        [summed[rows - 16 : rows - pad], summed[rows - pad :] + trail], axis=0
    ).astype(jnp.bfloat16)


def shards(tokens, nuc_table, short_filter, mr_filter, head_weight):
    rows = tokens.shape[0]
    channels = nuc_table.shape[2]
    filters, span = mr_filter.shape
    outs = head_weight.shape[2]
    seq_count = lax.axis_size("seq")
    vmem = pl.BlockSpec(memory_space=pltpu.VMEM)
    pad = 8
    return pl.pallas_call(
        functools.partial(kernel, seq_count),
        out_shape=jax.ShapeDtypeStruct((rows, outs), jnp.bfloat16),
        in_specs=[pl.BlockSpec(memory_space=pltpu.HBM)] * 5,
        out_specs=vmem,
        scratch_shapes=[
            pltpu.VMEM((1, rows), jnp.int32),
            pltpu.VMEM(nuc_table.shape, jnp.bfloat16),
            pltpu.VMEM(short_filter.shape, jnp.float32),
            pltpu.VMEM(mr_filter.shape, jnp.float32),
            pltpu.VMEM(head_weight.shape, jnp.bfloat16),
            pltpu.VMEM((filters, 2 * span, span), jnp.bfloat16),
            pltpu.VMEM((3, channels, 64), jnp.bfloat16),
            pltpu.VMEM((8, channels), jnp.float32),
            pltpu.VMEM((2, rows, channels), jnp.bfloat16),
            pltpu.VMEM((8, rows), jnp.int32),
            pltpu.VMEM((8, rows), jnp.int32),
            pltpu.VMEM((8, rows), jnp.int32),
            pltpu.VMEM((rows + 2 * pad, outs), jnp.float32),
            pltpu.VMEM((rows + 2 * pad, outs), jnp.float32),
            pltpu.VMEM((2, pad, outs), jnp.float32),
            pltpu.VMEM((2, pad, outs), jnp.float32),
            pltpu.SemaphoreType.DMA((5,)),
            pltpu.SemaphoreType.DMA((2,)),
            pltpu.SemaphoreType.DMA((2,)),
            pltpu.SemaphoreType.DMA((2,)),
            pltpu.SemaphoreType.DMA((2,)),
            pltpu.SemaphoreType.DMA((2, 2)),
            pltpu.SemaphoreType.DMA((2, 2)),
        ],
        compiler_params=pltpu.CompilerParams(
            collective_id=0, has_side_effects=True, vmem_limit_bytes=63 * 1024 * 1024
        ),
    )(tokens.reshape(1, rows), nuc_table, short_filter, mr_filter, head_weight)


def solution(mesh):
    in_specs = (
        P(("groups", "seq")),
        P(None, None, "ch"),
        P(None, None, "ch"),
        P("ch", None),
        P(None, "ch", None),
    )
    out_specs = P(("groups", "seq"), None)
    return jax.shard_map(shards, mesh=mesh, in_specs=in_specs, out_specs=out_specs, check_vma=False)
```

```python
import functools

import jax
import jax.numpy as jnp
from jax import lax
from jax.experimental import pallas as pl
from jax.experimental.pallas import tpu as pltpu
from jax.sharding import PartitionSpec as P

MESH = pl.DeviceIdType.MESH


def dot(lhs, rhs, lhs_dim=1, rhs_dim=0):
    return lax.dot_general(
        lhs, rhs, (((lhs_dim,), (rhs_dim,)), ((), ())), preferred_element_type=jnp.float32
    )


def kernel(
    seq_count, tok_hbm, nuc_hbm, short_hbm, mr_hbm, head_hbm, out_ref,
    tok_ref, nuc_ref, short_ref, mr_ref, head, toeplitz, taps, short8, track, own, left_tok, right_tok, total, other, left_sum, right_sum,
    load_sem, tok_send, tok_recv, sum_send, sum_recv, rim_send, rim_recv,
):
    rows = tok_ref.shape[1]
    filters, span = mr_ref.shape
    channels = nuc_ref.shape[2]
    short_len = short_ref.shape[1]
    head_taps, _, outs = head.shape
    rim = (head_taps - 1) // 2
    width = channels // filters
    letters_count = nuc_ref.shape[1]
    pad = 8
    group = lax.axis_index("groups")
    place = lax.axis_index("seq")
    core = lax.axis_index("ch")
    has_left = place > 0
    has_right = place < seq_count - 1
    left = place - 1
    right = place + 1

    barrier = pltpu.get_barrier_semaphore()
    pl.semaphore_signal(barrier, inc=1, device_id=(group, place, 1 - core), device_id_type=MESH)

    @pl.when(has_left)
    def _():
        for c in range(2):
            pl.semaphore_signal(barrier, inc=1, device_id=(group, left, c), device_id_type=MESH)

    @pl.when(has_right)
    def _():
        for c in range(2):
            pl.semaphore_signal(barrier, inc=1, device_id=(group, right, c), device_id_type=MESH)

    loads = [
        pltpu.make_async_copy(source, target, load_sem.at[n])
        for n, (source, target) in enumerate(
            [(tok_hbm, tok_ref), (short_hbm, short_ref), (nuc_hbm, nuc_ref), (mr_hbm, mr_ref), (head_hbm, head)]
        )
    ]
    for load in loads:
        load.start()
    loads[0].wait()
    own[...] = jnp.broadcast_to(tok_ref[...], own.shape)
    count = 1 + 2 * has_left.astype(jnp.int32) + 2 * has_right.astype(jnp.int32)
    pl.semaphore_wait(barrier, count)

    def tok_copy(side):
        return pltpu.make_async_remote_copy(
            src_ref=own,
            dst_ref=right_tok if side == 0 else left_tok,
            send_sem=tok_send.at[side],
            recv_sem=tok_recv.at[side],
            device_id=(group, left if side == 0 else right, core),
            device_id_type=MESH,
        )

    @pl.when(has_left)
    def _():
        tok_copy(0).start()

    @pl.when(has_right)
    def _():
        tok_copy(1).start()

    row_id = lax.broadcasted_iota(jnp.int32, (span, span), 0)
    lane_id = lax.broadcasted_iota(jnp.int32, (span, span), 1)

    loads[1].wait()
    loads[2].wait()
    for m in range(3):
        short8[m, 0:short_len, :] = short_ref[m]
        short8[m, short_len:8, :] = jnp.zeros((8 - short_len, channels), jnp.float32)

    def prepare(begin, end):
        at = slice(begin, end)
        for m in range(3):
            taps_f32 = short8[m, :, at]
            table = nuc_ref[m, :, at].astype(jnp.float32)
            full = jnp.concatenate([taps_f32 * table[n : n + 1] for n in range(letters_count)], axis=0)
            high = full.astype(jnp.bfloat16).astype(jnp.float32)
            both = jnp.concatenate([high, full - high], axis=0)
            taps[m, at, :] = both.T.astype(jnp.bfloat16)

    loads[3].wait()
    before = (lane_id < row_id).astype(jnp.bfloat16)

    part_channels = span
    part_count = channels // part_channels
    per_part = part_channels // width
    early_parts = part_count // 4
    prepare(0, early_parts * part_channels)

    def build(g):
        base = pltpu.roll(jnp.broadcast_to(mr_ref[pl.ds(g, 1), :], (8, span)), 0, 1, stride=1, stride_axis=0)
        turns = [base] + [pltpu.roll(base, n, 1) for n in range(8, span, 8)]
        circ = jnp.concatenate(turns, axis=0).astype(jnp.bfloat16)
        upper = circ * before
        toeplitz[g, 0:span] = upper
        toeplitz[g, span : 2 * span] = circ - upper

    def build_step(p, carry):
        for g in range(per_part):
            build(p * per_part + g)
        return carry

    lax.fori_loop(0, early_parts, build_step, 0)

    @pl.when(has_left)
    def _():
        tok_copy(1).wait_recv()

    @pl.when(has_right)
    def _():
        tok_copy(0).wait_recv()

    @pl.when(jnp.logical_not(has_left))
    def _():
        left_tok[...] = jnp.full(left_tok.shape, -1, jnp.int32)

    @pl.when(jnp.logical_not(has_right))
    def _():
        right_tok[...] = jnp.full(right_tok.shape, -1, jnp.int32)

    mid = own[...].astype(jnp.float32)
    ahead = jnp.concatenate([left_tok[...].astype(jnp.float32), mid], axis=1)
    behind = jnp.concatenate([mid, right_tok[...].astype(jnp.float32)], axis=1)
    behind = (letters_count - 1) - behind
    flip = (row_id + lane_id == span - 1).astype(jnp.bfloat16)
    pieces = [
        dot(behind[:, p * span : (p + 1) * span].astype(jnp.bfloat16), flip)
        for p in reversed(range(2 * rows // span))
    ]
    behind = jnp.concatenate(pieces, axis=1)
    hots = []
    for line in (ahead, behind):
        lags = pltpu.roll(line, 0, 1, stride=1, stride_axis=0)[:, rows - span :]
        hot = jnp.concatenate([(lags == n).astype(jnp.float32) for n in range(letters_count)], axis=0)
        hots.append(jnp.concatenate([hot, hot], axis=0).astype(jnp.bfloat16))
    reach = rows + span
    hot_all = jnp.concatenate(hots, axis=1)
    hot_query = jnp.concatenate([h[:, span:] for h in hots], axis=1)
    wide = 2 * span
    hot_tiles = [hot_all[:, t : t + wide] for t in range(0, 2 * reach, wide)]
    query_tiles = [hot_query[:, t : t + wide] for t in range(0, 2 * rows, wide)]
    blocks = rows // span
    perm_row = lax.broadcasted_iota(jnp.int32, (rows, rows), 0)
    perm_lane = lax.broadcasted_iota(jnp.int32, (rows, rows), 1)
    perms = [
        (perm_row == perm_lane).astype(jnp.bfloat16),
        (perm_row + perm_lane == rows - 1).astype(jnp.bfloat16),
    ]
    half = rows // 2

    def gate(p):
        at = slice(p * part_channels, (p + 1) * part_channels)
        cells = []
        for hot in hot_tiles:
            gated = (dot(taps[1, at, :], hot) * dot(taps[2, at, :], hot)).astype(jnp.bfloat16)
            cells += [gated[:, t : t + span] for t in range(0, hot.shape[1], span)]
        return cells

    def mix(p, cells):
        at = slice(p * part_channels, (p + 1) * part_channels)
        query = jnp.concatenate([dot(taps[0, at, :], hot) for hot in query_tiles], axis=1)
        parts = []
        for g in range(per_part):
            lines = slice(g * width, (g + 1) * width)
            stack = jnp.concatenate(
                [
                    jnp.concatenate(
                        [cells[s * (blocks + 1) + b][lines], cells[s * (blocks + 1) + b + 1][lines]], axis=1
                    )
                    for s in range(2)
                    for b in range(blocks)
                ],
                axis=0,
            )
            mixed = dot(stack, toeplitz[p * per_part + g])
            mixed = jnp.concatenate(
                [mixed[n * width : (n + 1) * width] for n in range(2 * blocks)], axis=1
            )
            parts.append((query[lines] * mixed).astype(jnp.bfloat16))
        return jnp.concatenate(parts, axis=0)

    def turn(begin, tracks):
        chunk_track = jnp.concatenate(tracks, axis=0)
        at = slice(begin * part_channels, (begin + len(tracks)) * part_channels)
        for s in range(2):
            turned = dot(perms[s], chunk_track[:, s * rows : (s + 1) * rows], 1, 1).astype(jnp.bfloat16)
            for h in range(2):
                track[h, s * half : (s + 1) * half, at] = turned[h * half : (h + 1) * half]

    pending = []
    cells = gate(0)
    for p in range(part_count):
        ahead_cells = gate(p + 1) if p + 1 < part_count else None
        if p + early_parts < part_count:
            prepare((p + early_parts) * part_channels, (p + early_parts + 1) * part_channels)
            for g in range(per_part):
                build((p + early_parts) * per_part + g)
        done = mix(p, cells)
        cells = ahead_cells
        pending.append(done)
        if len(pending) == 3:
            turn(p - 2, pending[:2])
            pending = pending[2:]
    turn(part_count - len(pending), pending)

    loads[4].wait()
    total[...] = jnp.zeros_like(total)
    cut = pad + half - 8

    def sum_copy(part):
        lines = pl.ds(pad, cut - pad) if part == 0 else pl.ds(cut, rows + pad - cut)
        return pltpu.make_async_remote_copy(
            src_ref=total.at[lines],
            dst_ref=other.at[lines],
            send_sem=sum_send.at[part],
            recv_sem=sum_recv.at[part],
            device_id=(group, place, 1 - core),
            device_id_type=MESH,
        )

    def rim_copy(side, c, from_core):
        begin = 0 if side == 0 else pad + rows
        slots = right_sum if side == 0 else left_sum
        return pltpu.make_async_remote_copy(
            src_ref=total.at[pl.ds(begin, pad)],
            dst_ref=slots.at[from_core],
            send_sem=rim_send.at[side, c],
            recv_sem=rim_recv.at[side, from_core],
            device_id=(group, left if side == 0 else right, c),
            device_id_type=MESH,
        )

    for part in range(2):
        for d in range(head_taps):
            term = dot(track[part], head[d])
            begin = pad + rim - d + part * half
            total[begin : begin + half, :] += term[:half]
            begin = pad + d - rim + part * half
            total[begin : begin + half, :] += term[half:]
        sum_copy(part).start()

        @pl.when(has_left if part == 0 else has_right)
        def _():
            for c in range(2):
                rim_copy(part, c, core).start()

    @pl.when(jnp.logical_not(has_left))
    def _():
        left_sum[...] = jnp.zeros_like(left_sum)

    @pl.when(jnp.logical_not(has_right))
    def _():
        right_sum[...] = jnp.zeros_like(right_sum)

    @pl.when(has_left)
    def _():
        tok_copy(0).wait_send()
        for c in range(2):
            rim_copy(0, c, core).wait_send()
            rim_copy(1, 0, c).wait_recv()

    @pl.when(has_right)
    def _():
        tok_copy(1).wait_send()
        for c in range(2):
            rim_copy(1, c, core).wait_send()
            rim_copy(0, 0, c).wait_recv()

    sum_copy(0).wait()
    sum_copy(1).wait()
    lead = left_sum[0] + left_sum[1]
    trail = right_sum[0] + right_sum[1]
    summed = total[pad : pad + rows, :] + other[pad : pad + rows, :]
    out_ref[0:16, :] = jnp.concatenate([summed[0:pad] + lead, summed[pad:16]], axis=0).astype(jnp.bfloat16)
    out_ref[16 : rows - 16, :] = summed[16 : rows - 16].astype(jnp.bfloat16)
    out_ref[rows - 16 : rows, :] = jnp.concatenate(
        [summed[rows - 16 : rows - pad], summed[rows - pad :] + trail], axis=0
    ).astype(jnp.bfloat16)


def shards(tokens, nuc_table, short_filter, mr_filter, head_weight):
    rows = tokens.shape[0]
    channels = nuc_table.shape[2]
    filters, span = mr_filter.shape
    outs = head_weight.shape[2]
    seq_count = lax.axis_size("seq")
    vmem = pl.BlockSpec(memory_space=pltpu.VMEM)
    pad = 8
    return pl.pallas_call(
        functools.partial(kernel, seq_count),
        out_shape=jax.ShapeDtypeStruct((rows, outs), jnp.bfloat16),
        in_specs=[pl.BlockSpec(memory_space=pltpu.HBM)] * 5,
        out_specs=vmem,
        scratch_shapes=[
            pltpu.VMEM((1, rows), jnp.int32),
            pltpu.VMEM(nuc_table.shape, jnp.bfloat16),
            pltpu.VMEM(short_filter.shape, jnp.float32),
            pltpu.VMEM(mr_filter.shape, jnp.float32),
            pltpu.VMEM(head_weight.shape, jnp.bfloat16),
            pltpu.VMEM((filters, 2 * span, span), jnp.bfloat16),
            pltpu.VMEM((3, channels, 64), jnp.bfloat16),
            pltpu.VMEM((3, 8, channels), jnp.float32),
            pltpu.VMEM((2, rows, channels), jnp.bfloat16),
            pltpu.VMEM((8, rows), jnp.int32),
            pltpu.VMEM((8, rows), jnp.int32),
            pltpu.VMEM((8, rows), jnp.int32),
            pltpu.VMEM((rows + 2 * pad, outs), jnp.float32),
            pltpu.VMEM((rows + 2 * pad, outs), jnp.float32),
            pltpu.VMEM((2, pad, outs), jnp.float32),
            pltpu.VMEM((2, pad, outs), jnp.float32),
            pltpu.SemaphoreType.DMA((5,)),
            pltpu.SemaphoreType.DMA((2,)),
            pltpu.SemaphoreType.DMA((2,)),
            pltpu.SemaphoreType.DMA((2,)),
            pltpu.SemaphoreType.DMA((2,)),
            pltpu.SemaphoreType.DMA((2, 2)),
            pltpu.SemaphoreType.DMA((2, 2)),
        ],
        compiler_params=pltpu.CompilerParams(
            collective_id=0, has_side_effects=True, vmem_limit_bytes=63 * 1024 * 1024
        ),
    )(tokens.reshape(1, rows), nuc_table, short_filter, mr_filter, head_weight)


def solution(mesh):
    in_specs = (
        P(("groups", "seq")),
        P(None, None, "ch"),
        P(None, None, "ch"),
        P("ch", None),
        P(None, "ch", None),
    )
    out_specs = P(("groups", "seq"), None)
    return jax.shard_map(shards, mesh=mesh, in_specs=in_specs, out_specs=out_specs, check_vma=False)
```

```python
import functools

import jax
import jax.numpy as jnp
from jax import lax
from jax.experimental import pallas as pl
from jax.experimental.pallas import tpu as pltpu
from jax.sharding import PartitionSpec as P

MESH = pl.DeviceIdType.MESH


def dot(lhs, rhs, lhs_dim=1, rhs_dim=0):
    return lax.dot_general(
        lhs, rhs, (((lhs_dim,), (rhs_dim,)), ((), ())), preferred_element_type=jnp.float32
    )


def kernel(
    seq_count, tok_hbm, nuc_hbm, short_hbm, mr_hbm, head_hbm, out_ref,
    tok_ref, nuc_ref, short_ref, mr_ref, head, toeplitz, taps, short8, track, own, left_tok, right_tok, total, other, left_sum, right_sum,
    load_sem, tok_send, tok_recv, sum_send, sum_recv, rim_send, rim_recv,
):
    rows = tok_ref.shape[1]
    filters, span = mr_ref.shape
    channels = nuc_ref.shape[2]
    short_len = short_ref.shape[1]
    head_taps, _, outs = head.shape
    rim = (head_taps - 1) // 2
    width = channels // filters
    letters_count = nuc_ref.shape[1]
    pad = 8
    group = lax.axis_index("groups")
    place = lax.axis_index("seq")
    core = lax.axis_index("ch")
    has_left = place > 0
    has_right = place < seq_count - 1
    left = place - 1
    right = place + 1

    barrier = pltpu.get_barrier_semaphore()
    pl.semaphore_signal(barrier, inc=1, device_id=(group, place, 1 - core), device_id_type=MESH)

    @pl.when(has_left)
    def _():
        for c in range(2):
            pl.semaphore_signal(barrier, inc=1, device_id=(group, left, c), device_id_type=MESH)

    @pl.when(has_right)
    def _():
        for c in range(2):
            pl.semaphore_signal(barrier, inc=1, device_id=(group, right, c), device_id_type=MESH)

    loads = [
        pltpu.make_async_copy(source, target, load_sem.at[n])
        for n, (source, target) in enumerate(
            [(tok_hbm, tok_ref), (short_hbm, short_ref), (nuc_hbm, nuc_ref), (mr_hbm, mr_ref), (head_hbm, head)]
        )
    ]
    for load in loads:
        load.start()
    loads[0].wait()
    own[...] = jnp.broadcast_to(tok_ref[...], own.shape)
    count = 1 + 2 * has_left.astype(jnp.int32) + 2 * has_right.astype(jnp.int32)
    pl.semaphore_wait(barrier, count)

    def tok_copy(side):
        return pltpu.make_async_remote_copy(
            src_ref=own,
            dst_ref=right_tok if side == 0 else left_tok,
            send_sem=tok_send.at[side],
            recv_sem=tok_recv.at[side],
            device_id=(group, left if side == 0 else right, core),
            device_id_type=MESH,
        )

    @pl.when(has_left)
    def _():
        tok_copy(0).start()

    @pl.when(has_right)
    def _():
        tok_copy(1).start()

    row_id = lax.broadcasted_iota(jnp.int32, (span, span), 0)
    lane_id = lax.broadcasted_iota(jnp.int32, (span, span), 1)

    loads[1].wait()
    loads[2].wait()
    for m in range(3):
        short8[m, 0:short_len, :] = short_ref[m]
        short8[m, short_len:8, :] = jnp.zeros((8 - short_len, channels), jnp.float32)

    def prepare(begin, end):
        at = slice(begin, end)
        for m in range(3):
            taps_f32 = short8[m, :, at]
            table = nuc_ref[m, :, at].astype(jnp.float32)
            full = jnp.concatenate([taps_f32 * table[n : n + 1] for n in range(letters_count)], axis=0)
            high = full.astype(jnp.bfloat16).astype(jnp.float32)
            both = jnp.concatenate([high, full - high], axis=0)
            taps[m, at, :] = both.T.astype(jnp.bfloat16)

    loads[3].wait()
    before = (lane_id < row_id).astype(jnp.bfloat16)

    part_channels = span
    part_count = channels // part_channels
    per_part = part_channels // width
    early_parts = part_count // 4
    prepare(0, early_parts * part_channels)

    def build(g):
        base = pltpu.roll(jnp.broadcast_to(mr_ref[pl.ds(g, 1), :], (8, span)), 0, 1, stride=1, stride_axis=0)
        turns = [base] + [pltpu.roll(base, n, 1) for n in range(8, span, 8)]
        circ = jnp.concatenate(turns, axis=0).astype(jnp.bfloat16)
        upper = circ * before
        toeplitz[g, 0:span] = upper
        toeplitz[g, span : 2 * span] = circ - upper

    def build_step(p, carry):
        for g in range(per_part):
            build(p * per_part + g)
        return carry

    lax.fori_loop(0, early_parts, build_step, 0)

    @pl.when(has_left)
    def _():
        tok_copy(1).wait_recv()

    @pl.when(has_right)
    def _():
        tok_copy(0).wait_recv()

    @pl.when(jnp.logical_not(has_left))
    def _():
        left_tok[...] = jnp.full(left_tok.shape, -1, jnp.int32)

    @pl.when(jnp.logical_not(has_right))
    def _():
        right_tok[...] = jnp.full(right_tok.shape, -1, jnp.int32)

    mid = own[...].astype(jnp.float32)
    ahead = jnp.concatenate([left_tok[...].astype(jnp.float32), mid], axis=1)
    behind = jnp.concatenate([mid, right_tok[...].astype(jnp.float32)], axis=1)
    behind = (letters_count - 1) - behind
    flip = (row_id + lane_id == span - 1).astype(jnp.bfloat16)
    pieces = [
        dot(behind[:, p * span : (p + 1) * span].astype(jnp.bfloat16), flip)
        for p in reversed(range(2 * rows // span))
    ]
    behind = jnp.concatenate(pieces, axis=1)
    hots = []
    for line in (ahead, behind):
        lags = pltpu.roll(line, 0, 1, stride=1, stride_axis=0)[:, rows - span :]
        hot = jnp.concatenate([(lags == n).astype(jnp.float32) for n in range(letters_count)], axis=0)
        hots.append(jnp.concatenate([hot, hot], axis=0).astype(jnp.bfloat16))
    reach = rows + span
    hot_all = jnp.concatenate(hots, axis=1)
    hot_query = jnp.concatenate([h[:, span:] for h in hots], axis=1)
    wide = 2 * span
    hot_tiles = [hot_all[:, t : t + wide] for t in range(0, 2 * reach, wide)]
    query_tiles = [hot_query[:, t : t + wide] for t in range(0, 2 * rows, wide)]
    blocks = rows // span
    perm_row = lax.broadcasted_iota(jnp.int32, (rows, rows), 0)
    perm_lane = lax.broadcasted_iota(jnp.int32, (rows, rows), 1)
    perms = [
        (perm_row == perm_lane).astype(jnp.bfloat16),
        (perm_row + perm_lane == rows - 1).astype(jnp.bfloat16),
    ]
    half = rows // 2

    def gate(p):
        at = slice(p * part_channels, (p + 1) * part_channels)
        cells = []
        for hot in hot_tiles:
            gated = (dot(taps[1, at, :], hot) * dot(taps[2, at, :], hot)).astype(jnp.bfloat16)
            cells += [gated[:, t : t + span] for t in range(0, hot.shape[1], span)]
        return cells

    def mix(p, cells):
        at = slice(p * part_channels, (p + 1) * part_channels)
        query = jnp.concatenate([dot(taps[0, at, :], hot) for hot in query_tiles], axis=1)
        parts = []
        for g in range(per_part):
            lines = slice(g * width, (g + 1) * width)
            stack = jnp.concatenate(
                [
                    jnp.concatenate(
                        [cells[s * (blocks + 1) + b][lines], cells[s * (blocks + 1) + b + 1][lines]], axis=1
                    )
                    for s in range(2)
                    for b in range(blocks)
                ],
                axis=0,
            )
            mixed = dot(stack, toeplitz[p * per_part + g])
            mixed = jnp.concatenate(
                [mixed[n * width : (n + 1) * width] for n in range(2 * blocks)], axis=1
            )
            parts.append((query[lines] * mixed).astype(jnp.bfloat16))
        return jnp.concatenate(parts, axis=0)

    def turn(begin, tracks):
        chunk_track = jnp.concatenate(tracks, axis=0)
        at = slice(begin * part_channels, (begin + len(tracks)) * part_channels)
        for s in range(2):
            turned = dot(perms[s], chunk_track[:, s * rows : (s + 1) * rows], 1, 1).astype(jnp.bfloat16)
            for h in range(2):
                track[h, s * half : (s + 1) * half, at] = turned[h * half : (h + 1) * half]

    def add_head(part, d, at):
        term = dot(track[part, :, at], head[d, at, :])
        begin = pad + rim - d + part * half
        total[begin : begin + half, :] += term[:half]
        begin = pad + d - rim + part * half
        total[begin : begin + half, :] += term[half:]

    total[...] = jnp.zeros_like(total)
    loads[4].wait()
    first = slice(0, channels // 2)
    second = slice(channels // 2, channels)
    jobs = [(part, d) for d in range(head_taps) for part in range(2)]
    pending = []
    cells = gate(0)
    for p in range(part_count):
        ahead_cells = gate(p + 1) if p + 1 < part_count else None
        if p + early_parts < part_count:
            prepare((p + early_parts) * part_channels, (p + early_parts + 1) * part_channels)
            for g in range(per_part):
                build((p + early_parts) * per_part + g)
        done = mix(p, cells)
        cells = ahead_cells
        pending.append(done)
        if len(pending) == 3:
            turn(p - 2, pending[:2])
            pending = pending[2:]
        if p > part_count // 2 + 1:
            for part, d in jobs[:2]:
                add_head(part, d, first)
            jobs = jobs[2:]
    turn(part_count - len(pending), pending)
    for part, d in jobs:
        add_head(part, d, first)

    cut = pad + half - 8

    def sum_copy(part):
        lines = pl.ds(pad, cut - pad) if part == 0 else pl.ds(cut, rows + pad - cut)
        return pltpu.make_async_remote_copy(
            src_ref=total.at[lines],
            dst_ref=other.at[lines],
            send_sem=sum_send.at[part],
            recv_sem=sum_recv.at[part],
            device_id=(group, place, 1 - core),
            device_id_type=MESH,
        )

    def rim_copy(side, c, from_core):
        begin = 0 if side == 0 else pad + rows
        slots = right_sum if side == 0 else left_sum
        return pltpu.make_async_remote_copy(
            src_ref=total.at[pl.ds(begin, pad)],
            dst_ref=slots.at[from_core],
            send_sem=rim_send.at[side, c],
            recv_sem=rim_recv.at[side, from_core],
            device_id=(group, left if side == 0 else right, c),
            device_id_type=MESH,
        )

    for part in range(2):
        for d in range(head_taps):
            add_head(part, d, second)
        sum_copy(part).start()

        @pl.when(has_left if part == 0 else has_right)
        def _():
            for c in range(2):
                rim_copy(part, c, core).start()

    @pl.when(jnp.logical_not(has_left))
    def _():
        left_sum[...] = jnp.zeros_like(left_sum)

    @pl.when(jnp.logical_not(has_right))
    def _():
        right_sum[...] = jnp.zeros_like(right_sum)

    @pl.when(has_left)
    def _():
        tok_copy(0).wait_send()
        for c in range(2):
            rim_copy(0, c, core).wait_send()
            rim_copy(1, 0, c).wait_recv()

    @pl.when(has_right)
    def _():
        tok_copy(1).wait_send()
        for c in range(2):
            rim_copy(1, c, core).wait_send()
            rim_copy(0, 0, c).wait_recv()

    sum_copy(0).wait()
    sum_copy(1).wait()
    lead = left_sum[0] + left_sum[1]
    trail = right_sum[0] + right_sum[1]
    summed = total[pad : pad + rows, :] + other[pad : pad + rows, :]
    out_ref[0:16, :] = jnp.concatenate([summed[0:pad] + lead, summed[pad:16]], axis=0).astype(jnp.bfloat16)
    out_ref[16 : rows - 16, :] = summed[16 : rows - 16].astype(jnp.bfloat16)
    out_ref[rows - 16 : rows, :] = jnp.concatenate(
        [summed[rows - 16 : rows - pad], summed[rows - pad :] + trail], axis=0
    ).astype(jnp.bfloat16)


def shards(tokens, nuc_table, short_filter, mr_filter, head_weight):
    rows = tokens.shape[0]
    channels = nuc_table.shape[2]
    filters, span = mr_filter.shape
    outs = head_weight.shape[2]
    seq_count = lax.axis_size("seq")
    vmem = pl.BlockSpec(memory_space=pltpu.VMEM)
    pad = 8
    return pl.pallas_call(
        functools.partial(kernel, seq_count),
        out_shape=jax.ShapeDtypeStruct((rows, outs), jnp.bfloat16),
        in_specs=[pl.BlockSpec(memory_space=pltpu.HBM)] * 5,
        out_specs=vmem,
        scratch_shapes=[
            pltpu.VMEM((1, rows), jnp.int32),
            pltpu.VMEM(nuc_table.shape, jnp.bfloat16),
            pltpu.VMEM(short_filter.shape, jnp.float32),
            pltpu.VMEM(mr_filter.shape, jnp.float32),
            pltpu.VMEM(head_weight.shape, jnp.bfloat16),
            pltpu.VMEM((filters, 2 * span, span), jnp.bfloat16),
            pltpu.VMEM((3, channels, 64), jnp.bfloat16),
            pltpu.VMEM((3, 8, channels), jnp.float32),
            pltpu.VMEM((2, rows, channels), jnp.bfloat16),
            pltpu.VMEM((8, rows), jnp.int32),
            pltpu.VMEM((8, rows), jnp.int32),
            pltpu.VMEM((8, rows), jnp.int32),
            pltpu.VMEM((rows + 2 * pad, outs), jnp.float32),
            pltpu.VMEM((rows + 2 * pad, outs), jnp.float32),
            pltpu.VMEM((2, pad, outs), jnp.float32),
            pltpu.VMEM((2, pad, outs), jnp.float32),
            pltpu.SemaphoreType.DMA((5,)),
            pltpu.SemaphoreType.DMA((2,)),
            pltpu.SemaphoreType.DMA((2,)),
            pltpu.SemaphoreType.DMA((2,)),
            pltpu.SemaphoreType.DMA((2,)),
            pltpu.SemaphoreType.DMA((2, 2)),
            pltpu.SemaphoreType.DMA((2, 2)),
        ],
        compiler_params=pltpu.CompilerParams(
            collective_id=0, has_side_effects=True, vmem_limit_bytes=63 * 1024 * 1024
        ),
    )(tokens.reshape(1, rows), nuc_table, short_filter, mr_filter, head_weight)


def solution(mesh):
    in_specs = (
        P(("groups", "seq")),
        P(None, None, "ch"),
        P(None, None, "ch"),
        P("ch", None),
        P(None, "ch", None),
    )
    out_specs = P(("groups", "seq"), None)
    return jax.shard_map(shards, mesh=mesh, in_specs=in_specs, out_specs=out_specs, check_vma=False)
```
